256 devices in a mesh: group: 2 (over y_lo), device: 128 (over z, y_hi, x, core).
Axes of the slice: x: 4, y: 4 (y_hi: 2, y_lo: 2; y = y_hi * 2 + y_lo), z: 8, core: 2. Of those that a mesh axis runs over, the one named last changes fastest.
Arguments:
- picture_encodings: bfloat16 [131072, 1152], P(('group', 'device')), as said below
- caption_span_encodings: bfloat16 [1024, 1152], P(('group', 'device')), as said below
- sharpness_factor: float32 [1], replicated, may hold values from 5 to 15
- score_shift_constant: float32 [1], replicated, may hold values from -3 to -1
Outputs:
- image_grad: float32 [131072, 1152], P(('group', 'device'))
- text_window_gradient: float32 [1024, 1152], P(('group', 'device'))
The draws below stay inside these ranges and needn't reach their ends.
Inputs may be any that keep to these rules, and one draw needn't show every extreme that they name: `picture_encodings`: each row has its own scale and each feature its own scale. `caption_span_encodings`: each row has its own scale and each feature its own scale.
All inputs are finite; a program needn't handle non-finite values.
Results may differ from the reference program's by a relative error of at most 0.0043.
Values may be sent and summed in bfloat16 or wider, within the bound.
No kernel may reach another device: no remote copies, remote signals or barrier semaphores. Data moves between devices by JAX's collectives and lax.ppermute only.
A program may use at most 64 MiB of HBM per device.

```python
import math
import jax
import jax.numpy as jnp
from jax import lax

D = 1152
ROWS = 512
TROWS = 4
BATCH = 131072
WINDOW = 1024


def scaled_rows(key, base, count):
    first, second = jax.random.split(key, 2)
    row_scale = jnp.exp(jax.random.uniform(first, (count, 1), jnp.float32, math.log(0.3), math.log(3.0)))
    col_scale = jnp.exp(jax.random.uniform(second, (1, D), jnp.float32, math.log(0.3), math.log(3.0)))
    return (base * row_scale * col_scale / math.sqrt(D)).astype(jnp.bfloat16)


def draw_picture_encodings(key, part):
    key = jax.random.fold_in(key, 11)
    scale_key, base_key = jax.random.split(key, 2)
    base = jnp.clip(jax.random.normal(base_key, (BATCH, D), jnp.float32), -6.0, 6.0)
    return scaled_rows(scale_key, base, BATCH)


def draw_caption_span_encodings(key, part):
    key = jax.random.fold_in(key, 23)
    scale_key, base_key = jax.random.split(key, 2)
    base = jnp.clip(jax.random.normal(base_key, (WINDOW, D), jnp.float32), -6.0, 6.0)
    return scaled_rows(scale_key, base, WINDOW)


def setup_inputs(seed: int = 0) -> dict:
    splits = jax.random.split(jax.random.key(seed), 5)
    picture_encodings = draw_picture_encodings(jax.random.fold_in(splits[4], 71), 0)
    caption_span_encodings = draw_caption_span_encodings(jax.random.fold_in(splits[4], 71), 0)
    sharpness_factor = jnp.clip(jax.random.uniform(splits[2], (1,), jnp.float32, 5.0, 15.0), 5.0, 15.0)
    score_shift_constant = jnp.clip(jax.random.uniform(splits[3], (1,), jnp.float32, -3.0, -1.0), -3.0, -1.0)
    return {"picture_encodings": picture_encodings, "caption_span_encodings": caption_span_encodings, "sharpness_factor": sharpness_factor, "score_shift_constant": score_shift_constant}


def normalized(embeds):
    values = embeds.astype(jnp.float32)
    inverse_norm = lax.rsqrt(lax.optimization_barrier(jnp.sum(values * values, axis=-1, keepdims=True)) + 1e-06)
    return (values * inverse_norm, inverse_norm)

def unit_backward(normed, inverse_norm, upstream):
    along = lax.optimization_barrier(jnp.sum(normed * upstream, axis=-1, keepdims=True))
    return inverse_norm * (upstream - normed * along)

def reference(picture_encodings, caption_span_encodings, sharpness_factor, score_shift_constant):
    image_unit, image_scale = normalized(picture_encodings)
    text_unit, text_scale = normalized(caption_span_encodings)
    picture_lower_bound = image_unit.astype(jnp.bfloat16)
    caption_lower_bound = text_unit.astype(jnp.bfloat16)
    score_sharpness = sharpness_factor[0].astype(jnp.float32)
    entry_displacement = score_shift_constant[0].astype(jnp.float32)
    block_rows = math.gcd(BATCH, 512)
    columns = jnp.arange(WINDOW, dtype=jnp.int32)
    column_labels = columns // TROWS * ROWS + columns % TROWS

    def single_block(text_acc, block_index):
        start = (block_index * block_rows).astype(jnp.int32)
        picture_tile = lax.dynamic_slice_in_dim(picture_lower_bound, start, block_rows, 0)
        similarity_scores = score_sharpness * jnp.dot(picture_tile, caption_lower_bound.T, preferred_element_type=jnp.float32) + entry_displacement
        row_ids = start + jnp.arange(block_rows, dtype=jnp.int32)
        diagonal = (row_ids[:, None] == column_labels[None, :]).astype(jnp.float32)
        couple_derivative = (jax.nn.sigmoid(similarity_scores) - diagonal).astype(jnp.bfloat16)
        picture_adjoint = score_sharpness * jnp.dot(couple_derivative, caption_lower_bound, preferred_element_type=jnp.float32)
        caption_portion = score_sharpness * jnp.dot(couple_derivative.T, picture_tile, preferred_element_type=jnp.float32)
        return (text_acc + caption_portion, picture_adjoint)
    text_back, image_blocks = lax.scan(single_block, jnp.zeros((WINDOW, D), jnp.float32), jnp.arange(BATCH // block_rows, dtype=jnp.int32))
    picture_adjoint = image_blocks.reshape(BATCH, D)
    image_grad = unit_backward(image_unit, image_scale, picture_adjoint)
    text_window_gradient = unit_backward(text_unit, text_scale, text_back)
    return (image_grad, text_window_gradient)
```

```python
import jax
import jax.numpy as jnp
from jax import lax
from jax.sharding import Mesh, PartitionSpec as P

ALL = ("yl", "z", "yh", "x", "c")
PLANE = ("yh", "yl", "x")
SWAP = [(0, 1), (1, 0)]


def normalized(embeds):
    values = embeds.astype(jnp.float32)
    inverse_norm = lax.rsqrt(jnp.sum(values * values, axis=-1, keepdims=True) + 1e-06)
    return (values * inverse_norm, inverse_norm)


def unit_backward(normed, inverse_norm, upstream):
    along = jnp.sum(normed * upstream, axis=-1, keepdims=True)
    return inverse_norm * (upstream - normed * along)


def exchange(block, axes):
    return lax.all_to_all(block, axes, 0, 0, tiled=True)


def spread(block, axes):
    n = lax.axis_size(axes)
    return exchange(jnp.broadcast_to(block[None], (n,) + block.shape), axes)


def pair_grad(images, texts, sharpness, shift):
    raw = jnp.einsum("rd,cd->rc", images, texts, preferred_element_type=jnp.float32)
    return jax.nn.sigmoid(sharpness * raw + shift)


def on_device(pictures, captions, sharpness_factor, score_shift_constant):
    sharpness, shift = sharpness_factor[0], score_shift_constant[0]
    trows, width = captions.shape
    nz, nxy = lax.axis_size("z"), lax.axis_size(PLANE)
    with jax.named_scope("gather_texts"):
        text_unit, text_scale = normalized(captions)
        line = spread(text_unit.astype(jnp.bfloat16), "z")
        texts = spread(line.reshape(nz * trows, width), PLANE).reshape(nxy * nz * trows, width)
    with jax.named_scope("images"):
        image_unit, image_scale = normalized(pictures)
        own = image_unit.astype(jnp.bfloat16)
        other = lax.ppermute(own, "c", SWAP)
    first = (lax.axis_index(PLANE) * nz + lax.axis_index("z")) * trows
    with jax.named_scope("pair_grad"):
        rows = lax.broadcasted_iota(jnp.int32, (own.shape[0], texts.shape[0]), 0)
        cols = lax.broadcasted_iota(jnp.int32, (own.shape[0], texts.shape[0]), 1)
        hit = (rows < trows) & (cols == first + rows)
        own_pair = (pair_grad(own, texts, sharpness, shift) - hit.astype(jnp.float32)).astype(jnp.bfloat16)
        other_pair = pair_grad(other, texts, sharpness, shift).astype(jnp.bfloat16)
    with jax.named_scope("text_back"):
        part = jnp.einsum("rc,rd->cd", own_pair, own, preferred_element_type=jnp.float32)
        part = part + jnp.einsum("rc,rd->cd", other_pair, other, preferred_element_type=jnp.float32)
        part = part.astype(jnp.bfloat16).reshape(nxy, nz * trows, width)
        part = jnp.sum(exchange(part, PLANE).astype(jnp.float32), axis=0)
        part = part.astype(jnp.bfloat16).reshape(nz, trows, width)
        text_back = sharpness * jnp.sum(exchange(part, "z").astype(jnp.float32), axis=0)
        text_grad = unit_backward(text_unit, text_scale, text_back)
    with jax.named_scope("image_back"):
        theirs = jnp.dot(other_pair, texts, preferred_element_type=jnp.float32)
        mine = jnp.dot(own_pair, texts, preferred_element_type=jnp.float32)
        image_back = sharpness * (mine + lax.ppermute(theirs, "c", SWAP))
        image_grad = unit_backward(image_unit, image_scale, image_back)
    return image_grad, text_grad


def solution(mesh):
    fine = Mesh(mesh.devices.reshape(2, 8, 2, 4, 2), ALL)
    whole = P(ALL, None)
    return jax.shard_map(
        on_device, mesh=fine, in_specs=(whole, whole, P(), P()), out_specs=(whole, whole), check_vma=False
    )
```

```python
import functools

import jax
import jax.numpy as jnp
from jax import lax
from jax.experimental import pallas as pl
from jax.experimental.pallas import tpu as pltpu
from jax.sharding import Mesh, PartitionSpec as P

ALL = ("yl", "z", "yh", "x", "c")
PLANE = ("yh", "yl", "x")
SWAP = [(0, 1), (1, 0)]
VMEM = pl.BlockSpec(memory_space=pltpu.VMEM)
SMEM = pl.BlockSpec(memory_space=pltpu.SMEM)
CONTRACT_LAST = (((1,), (1,)), ((), ()))


def normalized(embeds):
    values = embeds.astype(jnp.float32)
    inverse_norm = lax.rsqrt(jnp.sum(values * values, axis=-1, keepdims=True) + 1e-06)
    return (values * inverse_norm, inverse_norm)


def unit_backward(normed, inverse_norm, upstream):
    along = jnp.sum(normed * upstream, axis=-1, keepdims=True)
    return inverse_norm * (upstream - normed * along)


def call(kernel, outs, in_specs, args, flops=0, transcendentals=0, vmem=32 << 20):
    moved = sum(a.size * a.dtype.itemsize for a in args) + sum(o.size * o.dtype.itemsize for o in outs)
    return pl.pallas_call(
        kernel,
        out_shape=outs,
        in_specs=in_specs,
        out_specs=[VMEM] * len(outs),
        compiler_params=pltpu.CompilerParams(vmem_limit_bytes=vmem),
        cost_estimate=pl.CostEstimate(flops=flops, bytes_accessed=moved, transcendentals=transcendentals),
    )(*args)


def text_units(captions_ref, out_ref):
    low = normalized(captions_ref[...])[0].astype(jnp.bfloat16)
    for peer in range(out_ref.shape[0]):
        out_ref[peer] = low


def pair_terms(first_ref, sharpness_ref, shift_ref, texts_ref, own_ref, other_ref, part_ref, own_pair_ref, other_pair_ref, *, trows, tile):
    first, sharpness, shift = first_ref[0], sharpness_ref[0], shift_ref[0]
    for start in range(0, texts_ref.shape[0], tile):
        block = pl.ds(start, tile)
        texts = texts_ref[block, :]
        raw = lax.dot_general(texts, own_ref[...], CONTRACT_LAST, preferred_element_type=jnp.float32)
        grad = 1.0 / (1.0 + jnp.exp(-(sharpness * raw + shift)))
        text = start - first + lax.broadcasted_iota(jnp.int32, raw.shape, 0)
        image = lax.broadcasted_iota(jnp.int32, raw.shape, 1)
        grad = jnp.where((text == image) & (image < trows), grad - 1.0, grad).astype(jnp.bfloat16)
        own_pair_ref[block, :] = grad
        part = jnp.dot(grad, own_ref[...], preferred_element_type=jnp.float32)
        raw = lax.dot_general(texts, other_ref[...], CONTRACT_LAST, preferred_element_type=jnp.float32)
        grad = (1.0 / (1.0 + jnp.exp(-(sharpness * raw + shift)))).astype(jnp.bfloat16)
        other_pair_ref[block, :] = grad
        part = part + jnp.dot(grad, other_ref[...], preferred_element_type=jnp.float32)
        part_ref[block, :] = part.astype(jnp.bfloat16)


def plane_sum(parts_ref, out_ref):
    total = parts_ref[0].astype(jnp.float32)
    for peer in range(1, parts_ref.shape[0]):
        total = total + parts_ref[peer].astype(jnp.float32)
    trows = out_ref.shape[1]
    for peer in range(out_ref.shape[0]):
        out_ref[peer] = total[peer * trows : (peer + 1) * trows].astype(jnp.bfloat16)


def text_finish(sharpness_ref, parts_ref, captions_ref, out_ref):
    total = parts_ref[0].astype(jnp.float32)
    for peer in range(1, parts_ref.shape[0]):
        total = total + parts_ref[peer].astype(jnp.float32)
    unit, scale = normalized(captions_ref[...])
    out_ref[...] = unit_backward(unit, scale, sharpness_ref[0] * total)


def exchange(block, axes):
    return lax.all_to_all(block, axes, 0, 0, tiled=True)


def on_device(pictures, captions, sharpness_factor, score_shift_constant):
    trows, width = captions.shape
    rows = pictures.shape[0]
    nz, nxy = lax.axis_size("z"), lax.axis_size(PLANE)
    ntexts = nxy * nz * trows
    bf16, f32 = jnp.bfloat16, jnp.float32
    shaped = jax.ShapeDtypeStruct
    with jax.named_scope("gather_texts"):
        (line,) = call(text_units, [shaped((nz, trows, width), bf16)], [VMEM], [captions])
        line = exchange(line, "z").reshape(nz * trows, width)
        texts = exchange(jnp.broadcast_to(line[None], (nxy,) + line.shape), PLANE).reshape(ntexts, width)
    with jax.named_scope("images"):
        image_unit, image_scale = normalized(pictures)
        own = image_unit.astype(bf16)
        other = lax.ppermute(own, "c", SWAP)
    first = (lax.axis_index(PLANE) * nz + lax.axis_index("z")) * trows
    with jax.named_scope("pair_terms"):
        part, own_pair, other_pair = call(
            functools.partial(pair_terms, trows=trows, tile=256),
            [shaped((ntexts, width), bf16), shaped((ntexts, rows), bf16), shaped((ntexts, rows), bf16)],
            [SMEM] * 3 + [VMEM] * 3,
            [first.astype(jnp.int32).reshape(1), sharpness_factor, score_shift_constant, texts, own, other],
            flops=8 * ntexts * rows * width,
            transcendentals=2 * ntexts * rows,
        )
    with jax.named_scope("text_back"):
        parts = exchange(part.reshape(nxy, nz * trows, width), PLANE)
        (line,) = call(plane_sum, [shaped((nz, trows, width), bf16)], [VMEM], [parts])
        (text_grad,) = call(
            text_finish,
            [shaped((trows, width), f32)],
            [SMEM, VMEM, VMEM],
            [sharpness_factor, exchange(line, "z"), captions],
        )
    with jax.named_scope("image_back"):
        theirs = jnp.einsum("cr,cd->rd", other_pair, texts, preferred_element_type=f32)
        mine = jnp.einsum("cr,cd->rd", own_pair, texts, preferred_element_type=f32)
        image_back = sharpness_factor[0] * (mine + lax.ppermute(theirs, "c", SWAP))
        image_grad = unit_backward(image_unit, image_scale, image_back)
    return image_grad, text_grad


def solution(mesh):
    fine = Mesh(mesh.devices.reshape(2, 8, 2, 4, 2), ALL)
    whole = P(ALL, None)
    return jax.shard_map(
        on_device, mesh=fine, in_specs=(whole, whole, P(), P()), out_specs=(whole, whole), check_vma=False
    )
```

```python
import functools

import jax
import jax.numpy as jnp
import numpy as np
from jax import lax
from jax.experimental import pallas as pl
from jax.experimental.pallas import tpu as pltpu
from jax.sharding import Mesh, PartitionSpec as P

VMEM = pl.BlockSpec(memory_space=pltpu.VMEM)
ANY = pl.BlockSpec(memory_space=pl.ANY)
SMEM = pl.BlockSpec(memory_space=pltpu.SMEM)
CONTRACT_LAST = (((1,), (1,)), ((), ()))
BF16, F32 = jnp.bfloat16, jnp.float32
LINE = 4


def normalized(embeds):
    values = embeds.astype(F32)
    inverse_norm = lax.rsqrt(jnp.sum(values * values, axis=-1, keepdims=True) + 1e-06)
    return (values * inverse_norm, inverse_norm)


def unit_backward(normed, inverse_norm, upstream):
    along = jnp.sum(normed * upstream, axis=-1, keepdims=True)
    return inverse_norm * (upstream - normed * along)


def call(kernel, outs, in_specs, args, flops=0, transcendentals=0, vmem=16 << 20, **more):
    moved = sum(a.size * a.dtype.itemsize for a in args) + sum(o.size * o.dtype.itemsize for o in outs)
    more.setdefault("out_specs", [VMEM] * len(outs))
    return pl.pallas_call(
        kernel,
        out_shape=outs,
        in_specs=in_specs,
        compiler_params=pltpu.CompilerParams(vmem_limit_bytes=vmem),
        cost_estimate=pl.CostEstimate(flops=flops, bytes_accessed=moved, transcendentals=transcendentals),
        **more,
    )(*args)


def text_units(captions_ref, out_ref):
    low = normalized(captions_ref[...])[0].astype(BF16)
    for peer in range(out_ref.shape[0]):
        out_ref[peer] = low


def place_in_sheet(device):
    y, z, x = 2 * (device // 8 % 2) + device // 128, device // 16 % 8, device // 2 % 4
    return 4 * z + jnp.where(device % 2 == 0, y, x)


def sigmoids(rows, columns, sharpness, shift):
    raw = lax.dot_general(rows, columns, CONTRACT_LAST, preferred_element_type=F32)
    return 1.0 / (1.0 + jnp.exp(-(sharpness * raw + shift)))


def less_pairs(grad, image_axis, first, trows):
    image = lax.broadcasted_iota(jnp.int32, grad.shape, image_axis)
    text = lax.broadcasted_iota(jnp.int32, grad.shape, 1 - image_axis) - first
    return jnp.where((text == image) & (image < trows), grad - 1.0, grad)


def own_terms(device_ref, sharpness_ref, shift_ref, texts_ref, pictures_ref, partner_ref, part_ref, own_ref, other_ref, raw, sems, *, trows):
    sharpness, shift = sharpness_ref[0], shift_ref[0]
    reads = [pltpu.make_async_copy(ref, raw.at[k], sems.at[k]) for k, ref in enumerate((pictures_ref, partner_ref))]
    for read in reads:
        read.start()
    texts = texts_ref[...]
    reads[0].wait()
    own = normalized(raw[0])[0].astype(BF16)
    own_ref[...] = own
    grad = sigmoids(texts, own, sharpness, shift)
    grad = less_pairs(grad, 1, trows * place_in_sheet(device_ref[0]), trows).astype(BF16)
    part = jnp.dot(grad, own, preferred_element_type=F32)
    reads[1].wait()
    other = normalized(raw[1])[0].astype(BF16)
    other_ref[...] = other
    grad = sigmoids(texts, other, sharpness, shift).astype(BF16)
    part_ref[...] = part + jnp.dot(grad, other, preferred_element_type=F32)


def far_terms(sharpness_ref, shift_ref, own_ref, other_ref, *refs):
    sharpness, shift = sharpness_ref[0], shift_ref[0]
    n = len(refs) // 2
    rows = refs[0].shape[0]
    texts = jnp.concatenate([ref[...] for ref in refs[:n]], axis=0)
    grad = sigmoids(texts, own_ref[...], sharpness, shift).astype(BF16)
    part = jnp.dot(grad, own_ref[...], preferred_element_type=F32)
    grad = sigmoids(texts, other_ref[...], sharpness, shift).astype(BF16)
    part = part + jnp.dot(grad, other_ref[...], preferred_element_type=F32)
    for k in range(n):
        refs[n + k][...] = part[k * rows : (k + 1) * rows].astype(BF16)


def near_sum(own_ref, left_ref, right_ref, out_ref):
    out_ref[...] = own_ref[...] + left_ref[...].astype(F32) + right_ref[...].astype(F32)


def image_finish(device_ref, sharpness_ref, shift_ref, pictures_ref, *refs, trows):
    sharpness, shift = sharpness_ref[0], shift_ref[0]
    blocks = refs[: 2 * LINE]
    out_ref, raw, held, read_sem, sems = refs[2 * LINE :]
    read = pltpu.make_async_copy(pictures_ref, raw, read_sem)
    read.start()
    texts = jnp.concatenate([ref[...] for ref in blocks], axis=0)
    read.wait()
    tiles, tile = held.shape[:2]
    copies = []
    for k in range(tiles):
        rows = pl.ds(k * tile, tile)
        unit, scale = normalized(raw[rows, :])
        grad = sigmoids(unit.astype(BF16), texts, sharpness, shift)
        if k * tile < trows:
            grad = less_pairs(grad, 0, trows * place_in_sheet(device_ref[0]), trows)
        back = jnp.dot(grad.astype(BF16), texts, preferred_element_type=F32)
        held[k] = unit_backward(unit, scale, sharpness * back)
        copy = pltpu.make_async_copy(held.at[k], out_ref.at[rows, :], sems.at[k])
        copy.start()
        copies.append(copy)
    for copy in copies:
        copy.wait()


def line_sum(own_ref, *refs):
    out_ref = refs[-1]
    total = own_ref[...]
    for ref in refs[:-1]:
        total = total + ref[...].astype(F32)
    trows = out_ref.shape[1]
    for peer in range(out_ref.shape[0]):
        out_ref[peer] = total[peer * trows : (peer + 1) * trows].astype(BF16)


def text_finish(sharpness_ref, parts_ref, captions_ref, out_ref):
    total = parts_ref[0].astype(F32)
    for peer in range(1, parts_ref.shape[0]):
        total = total + parts_ref[peer].astype(F32)
    unit, scale = normalized(captions_ref[...])
    out_ref[...] = unit_backward(unit, scale, sharpness_ref[0] * total)


def routes():
    number = np.arange(256).reshape(2, 8, 2, 4, 2).transpose(4, 1, 2, 0, 3).reshape(2, 8, 4, 4)
    sheets = [number[0, :, :, x].reshape(-1) for x in range(4)] + [number[1, :, y, :].reshape(-1) for y in range(4)]
    lines = []
    for k in range(LINE):
        ahead = np.stack([np.roll(number[0], -k, axis=2), np.roll(number[1], -k, axis=1)])
        lines.append([(int(a), int(b)) for a, b in zip(number.reshape(-1), ahead.reshape(-1))])
    swap = [(int(i), int(i) ^ 1) for i in range(256)]
    return [[int(i) for i in sheet] for sheet in sheets], lines, swap


def on_device(pictures, captions, sharpness_factor, score_shift_constant):
    sheets, lines, swap = routes()
    trows, width = captions.shape
    rows = pictures.shape[0]
    n = len(sheets[0])
    block = n * trows
    shaped = jax.ShapeDtypeStruct

    def exchange(parts):
        return lax.all_to_all(parts, "d", 0, 0, axis_index_groups=sheets, tiled=True)

    with jax.named_scope("gather_texts"):
        partner = lax.ppermute(pictures, "d", swap)
        (sheet,) = call(text_units, [shaped((n, trows, width), BF16)], [VMEM], [captions])
        near = exchange(sheet).reshape(block, width)
        far = [lax.ppermute(near, "d", lines[k]) for k in (1, 3, 2)]
        beside = [lax.ppermute(texts, "d", swap) for texts in (near, *far)]
    device = lax.axis_index("d").astype(jnp.int32).reshape(1)
    scalars = [sharpness_factor, score_shift_constant]
    low, part = shaped((rows, width), BF16), shaped((block, width), BF16)
    work = dict(flops=8 * block * rows * width, transcendentals=2 * block * rows)
    with jax.named_scope("own_terms"):
        near_part, own, other = call(
            functools.partial(own_terms, trows=trows),
            [shaped((block, width), F32), low, low],
            [SMEM] * 3 + [VMEM, ANY, ANY],
            [device, *scalars, near, pictures, partner],
            scratch_shapes=[pltpu.VMEM((2, rows, width), BF16), pltpu.SemaphoreType.DMA((2,))],
            **work,
        )
    with jax.named_scope("far_terms"):
        p1, p3 = call(far_terms, [part] * 2, [SMEM] * 2 + [VMEM] * 4, [*scalars, own, other, far[0], far[1]], **work)
        back = [lax.ppermute(p1, "d", lines[3]), lax.ppermute(p3, "d", lines[1])]
        p1, far[2] = lax.optimization_barrier((p1, far[2]))
        (p2,) = call(far_terms, [part], [SMEM] * 2 + [VMEM] * 3, [*scalars, own, other, far[2]], **work)
        back += [lax.ppermute(p2, "d", lines[2])]
    with jax.named_scope("text_back"):
        (near_part,) = call(near_sum, [shaped((block, width), F32)], [VMEM] * 3, [near_part, *back[:2]])
        (total,) = call(line_sum, [shaped((n, trows, width), BF16)], [VMEM] * 2, [near_part, back[2]])
        sheet = exchange(total)
    with jax.named_scope("image_back"):
        tiles = 2
        (image_grad,) = call(
            functools.partial(image_finish, trows=trows),
            [shaped((rows, width), F32)],
            [SMEM] * 3 + [ANY] + [VMEM] * 8,
            [device, *scalars, pictures, near, *far, *beside],
            flops=16 * LINE * block * rows * width // 2,
            out_specs=[ANY],
            scratch_shapes=[
                pltpu.VMEM((rows, width), BF16),
                pltpu.VMEM((tiles, rows // tiles, width), F32),
                pltpu.SemaphoreType.DMA,
                pltpu.SemaphoreType.DMA((tiles,)),
            ],
        )
    with jax.named_scope("text_finish"):
        sheet, image_grad = lax.optimization_barrier((sheet, image_grad))
        (text_grad,) = call(
            text_finish,
            [shaped((trows, width), F32)],
            [SMEM, VMEM, VMEM],
            [sharpness_factor, sheet, captions],
        )
    return image_grad, text_grad


def solution(mesh):
    flat = Mesh(mesh.devices.reshape(-1), ("d",))
    whole = P("d", None)
    return jax.shard_map(
        on_device, mesh=flat, in_specs=(whole, whole, P(), P()), out_specs=(whole, whole), check_vma=False
    )
```

```python
import functools

import jax
import jax.numpy as jnp
import numpy as np
from jax import lax
from jax.experimental import pallas as pl
from jax.experimental.pallas import tpu as pltpu
from jax.sharding import Mesh, PartitionSpec as P

VMEM = pl.BlockSpec(memory_space=pltpu.VMEM)
ANY = pl.BlockSpec(memory_space=pl.ANY)
SMEM = pl.BlockSpec(memory_space=pltpu.SMEM)
CONTRACT_LAST = (((1,), (1,)), ((), ()))
BF16, F32 = jnp.bfloat16, jnp.float32
LINE = 4


def normalized(embeds):
    values = embeds.astype(F32)
    inverse_norm = lax.rsqrt(jnp.sum(values * values, axis=-1, keepdims=True) + 1e-06)
    return (values * inverse_norm, inverse_norm)


def unit_backward(normed, inverse_norm, upstream):
    along = jnp.sum(normed * upstream, axis=-1, keepdims=True)
    return inverse_norm * (upstream - normed * along)


def call(kernel, outs, in_specs, args, flops=0, transcendentals=0, vmem=16 << 20, **more):
    moved = sum(a.size * a.dtype.itemsize for a in args) + sum(o.size * o.dtype.itemsize for o in outs)
    more.setdefault("out_specs", [VMEM] * len(outs))
    return pl.pallas_call(
        kernel,
        out_shape=outs,
        in_specs=in_specs,
        compiler_params=pltpu.CompilerParams(vmem_limit_bytes=vmem),
        cost_estimate=pl.CostEstimate(flops=flops, bytes_accessed=moved, transcendentals=transcendentals),
        **more,
    )(*args)


def text_units(captions_ref, out_ref):
    low = normalized(captions_ref[...])[0].astype(BF16)
    for peer in range(out_ref.shape[0]):
        out_ref[peer] = low


def place_in_sheet(device):
    y, z, x = 2 * (device // 8 % 2) + device // 128, device // 16 % 8, device // 2 % 4
    return 4 * z + jnp.where(device % 2 == 0, y, x)


def sigmoids(rows, columns, sharpness, shift):
    raw = lax.dot_general(rows, columns, CONTRACT_LAST, preferred_element_type=F32)
    return 1.0 / (1.0 + jnp.exp(-(sharpness * raw + shift)))


def less_pairs(grad, image_axis, first, trows):
    image = lax.broadcasted_iota(jnp.int32, grad.shape, image_axis)
    text = lax.broadcasted_iota(jnp.int32, grad.shape, 1 - image_axis) - first
    return jnp.where((text == image) & (image < trows), grad - 1.0, grad)


def own_terms(device_ref, sharpness_ref, shift_ref, texts_ref, pictures_ref, partner_ref, part_ref, own_ref, other_ref, raw, sems, *, trows):
    sharpness, shift = sharpness_ref[0], shift_ref[0]
    reads = [pltpu.make_async_copy(ref, raw.at[k], sems.at[k]) for k, ref in enumerate((pictures_ref, partner_ref))]
    for read in reads:
        read.start()
    texts = texts_ref[...]
    reads[0].wait()
    own = normalized(raw[0])[0].astype(BF16)
    own_ref[...] = own
    grad = sigmoids(texts, own, sharpness, shift)
    grad = less_pairs(grad, 1, trows * place_in_sheet(device_ref[0]), trows).astype(BF16)
    part = jnp.dot(grad, own, preferred_element_type=F32)
    reads[1].wait()
    other = normalized(raw[1])[0].astype(BF16)
    other_ref[...] = other
    grad = sigmoids(texts, other, sharpness, shift).astype(BF16)
    part_ref[...] = part + jnp.dot(grad, other, preferred_element_type=F32)


def far_terms(sharpness_ref, shift_ref, own_ref, other_ref, *refs):
    sharpness, shift = sharpness_ref[0], shift_ref[0]
    n = len(refs) // 2
    rows = refs[0].shape[0]
    texts = jnp.concatenate([ref[...] for ref in refs[:n]], axis=0)
    grad = sigmoids(texts, own_ref[...], sharpness, shift).astype(BF16)
    part = jnp.dot(grad, own_ref[...], preferred_element_type=F32)
    grad = sigmoids(texts, other_ref[...], sharpness, shift).astype(BF16)
    part = part + jnp.dot(grad, other_ref[...], preferred_element_type=F32)
    for k in range(n):
        refs[n + k][...] = part[k * rows : (k + 1) * rows].astype(BF16)


def near_sum(own_ref, far_ref, out_ref):
    out_ref[...] = own_ref[...] + far_ref[...].astype(F32)


def image_finish(device_ref, sharpness_ref, shift_ref, pictures_ref, *refs, trows):
    sharpness, shift = sharpness_ref[0], shift_ref[0]
    blocks = refs[: 2 * LINE]
    out_ref, raw, held, read_sem, sems = refs[2 * LINE :]
    read = pltpu.make_async_copy(pictures_ref, raw, read_sem)
    read.start()
    texts = jnp.concatenate([ref[...] for ref in blocks], axis=0)
    read.wait()
    tiles, tile = held.shape[:2]
    copies = []
    for k in range(tiles):
        rows = pl.ds(k * tile, tile)
        unit, scale = normalized(raw[rows, :])
        grad = sigmoids(unit.astype(BF16), texts, sharpness, shift)
        if k * tile < trows:
            grad = less_pairs(grad, 0, trows * place_in_sheet(device_ref[0]), trows)
        back = jnp.dot(grad.astype(BF16), texts, preferred_element_type=F32)
        held[k] = unit_backward(unit, scale, sharpness * back)
        copy = pltpu.make_async_copy(held.at[k], out_ref.at[rows, :], sems.at[k])
        copy.start()
        copies.append(copy)
    for copy in copies:
        copy.wait()


def line_sum(own_ref, *refs):
    out_ref = refs[-1]
    total = own_ref[...]
    for ref in refs[:-1]:
        total = total + ref[...].astype(F32)
    trows = out_ref.shape[1]
    for peer in range(out_ref.shape[0]):
        out_ref[peer] = total[peer * trows : (peer + 1) * trows].astype(BF16)


def text_finish(sharpness_ref, parts_ref, captions_ref, out_ref):
    total = parts_ref[0].astype(F32)
    for peer in range(1, parts_ref.shape[0]):
        total = total + parts_ref[peer].astype(F32)
    unit, scale = normalized(captions_ref[...])
    out_ref[...] = unit_backward(unit, scale, sharpness_ref[0] * total)


def routes():
    number = np.arange(256).reshape(2, 8, 2, 4, 2).transpose(4, 1, 2, 0, 3).reshape(2, 8, 4, 4)
    sheets = [number[0, :, :, x].reshape(-1) for x in range(4)] + [number[1, :, y, :].reshape(-1) for y in range(4)]
    lines = []
    for k in range(LINE):
        ahead = np.stack([np.roll(number[0], -k, axis=2), np.roll(number[1], -k, axis=1)])
        lines.append([(int(a), int(b)) for a, b in zip(number.reshape(-1), ahead.reshape(-1))])
    swap = [(int(i), int(i) ^ 1) for i in range(256)]
    return [[int(i) for i in sheet] for sheet in sheets], lines, swap


def on_device(pictures, captions, sharpness_factor, score_shift_constant):
    sheets, lines, swap = routes()
    trows, width = captions.shape
    rows = pictures.shape[0]
    n = len(sheets[0])
    block = n * trows
    shaped = jax.ShapeDtypeStruct

    def exchange(parts):
        return lax.all_to_all(parts, "d", 0, 0, axis_index_groups=sheets, tiled=True)

    with jax.named_scope("gather_texts"):
        partner = lax.ppermute(pictures, "d", swap)
        (sheet,) = call(text_units, [shaped((n, trows, width), BF16)], [VMEM], [captions])
        near = exchange(sheet).reshape(block, width)
        far = [lax.ppermute(near, "d", lines[k]) for k in (2, 1, 3)]
        far = far[1:] + far[:1]
        beside = [lax.ppermute(texts, "d", swap) for texts in (near, *far)]
    device = lax.axis_index("d").astype(jnp.int32).reshape(1)
    scalars = [sharpness_factor, score_shift_constant]
    low, part = shaped((rows, width), BF16), shaped((block, width), BF16)
    work = dict(flops=8 * block * rows * width, transcendentals=2 * block * rows)
    with jax.named_scope("own_terms"):
        near_part, own, other = call(
            functools.partial(own_terms, trows=trows),
            [shaped((block, width), F32), low, low],
            [SMEM] * 3 + [VMEM, ANY, ANY],
            [device, *scalars, near, pictures, partner],
            scratch_shapes=[pltpu.VMEM((2, rows, width), BF16), pltpu.SemaphoreType.DMA((2,))],
            **work,
        )
    with jax.named_scope("far_terms"):
        (p2,) = call(far_terms, [part], [SMEM] * 2 + [VMEM] * 3, [*scalars, own, other, far[2]], **work)
        back = [lax.ppermute(p2, "d", lines[2])]
        p2, far[0] = lax.optimization_barrier((p2, far[0]))
        p1, p3 = call(far_terms, [part] * 2, [SMEM] * 2 + [VMEM] * 4, [*scalars, own, other, far[0], far[1]], **work)
        back += [lax.ppermute(p1, "d", lines[3]), lax.ppermute(p3, "d", lines[1])]
    with jax.named_scope("text_back"):
        (near_part,) = call(near_sum, [shaped((block, width), F32)], [VMEM] * 2, [near_part, back[0]])
        (total,) = call(line_sum, [shaped((n, trows, width), BF16)], [VMEM] * 3, [near_part, *back[1:]])
        sheet = exchange(total)
    with jax.named_scope("image_back"):
        tiles = 2
        (image_grad,) = call(
            functools.partial(image_finish, trows=trows),
            [shaped((rows, width), F32)],
            [SMEM] * 3 + [ANY] + [VMEM] * 8,
            [device, *scalars, pictures, near, *far, *beside],
            flops=16 * LINE * block * rows * width // 2,
            out_specs=[ANY],
            scratch_shapes=[
                pltpu.VMEM((rows, width), BF16),
                pltpu.VMEM((tiles, rows // tiles, width), F32),
                pltpu.SemaphoreType.DMA,
                pltpu.SemaphoreType.DMA((tiles,)),
            ],
        )
    with jax.named_scope("text_finish"):
        sheet, image_grad = lax.optimization_barrier((sheet, image_grad))
        (text_grad,) = call(
            text_finish,
            [shaped((trows, width), F32)],
            [SMEM, VMEM, VMEM],
            [sharpness_factor, sheet, captions],
        )
    return image_grad, text_grad


def solution(mesh):
    flat = Mesh(mesh.devices.reshape(-1), ("d",))
    whole = P("d", None)
    return jax.shard_map(
        on_device, mesh=flat, in_specs=(whole, whole, P(), P()), out_specs=(whole, whole), check_vma=False
    )
```

```python
import functools

import jax
import jax.numpy as jnp
import numpy as np
from jax import lax
from jax.experimental import pallas as pl
from jax.experimental.pallas import tpu as pltpu
from jax.sharding import Mesh, PartitionSpec as P

VMEM = pl.BlockSpec(memory_space=pltpu.VMEM)
ANY = pl.BlockSpec(memory_space=pl.ANY)
SMEM = pl.BlockSpec(memory_space=pltpu.SMEM)
CONTRACT_LAST = (((1,), (1,)), ((), ()))
BF16, F32 = jnp.bfloat16, jnp.float32
LINE = 4


def normalized(embeds):
    values = embeds.astype(F32)
    inverse_norm = lax.rsqrt(jnp.sum(values * values, axis=-1, keepdims=True) + 1e-06)
    return (values * inverse_norm, inverse_norm)


def unit_backward(normed, inverse_norm, upstream):
    along = jnp.sum(normed * upstream, axis=-1, keepdims=True)
    return inverse_norm * (upstream - normed * along)


def call(kernel, outs, in_specs, args, flops=0, transcendentals=0, vmem=16 << 20, **more):
    moved = sum(a.size * a.dtype.itemsize for a in args) + sum(o.size * o.dtype.itemsize for o in outs)
    more.setdefault("out_specs", [VMEM] * len(outs))
    return pl.pallas_call(
        kernel,
        out_shape=outs,
        in_specs=in_specs,
        compiler_params=pltpu.CompilerParams(vmem_limit_bytes=vmem),
        cost_estimate=pl.CostEstimate(flops=flops, bytes_accessed=moved, transcendentals=transcendentals),
        **more,
    )(*args)


def text_units(captions_ref, out_ref):
    low = normalized(captions_ref[...])[0].astype(BF16)
    for peer in range(out_ref.shape[0]):
        out_ref[peer] = low


def place_in_sheet(device):
    y, z, x = 2 * (device // 8 % 2) + device // 128, device // 16 % 8, device // 2 % 4
    return 4 * z + jnp.where(device % 2 == 0, y, x)


def sigmoids(rows, columns, sharpness, shift):
    raw = lax.dot_general(rows, columns, CONTRACT_LAST, preferred_element_type=F32)
    return 1.0 / (1.0 + jnp.exp(-(sharpness * raw + shift)))


def less_pairs(grad, image_axis, first, trows):
    image = lax.broadcasted_iota(jnp.int32, grad.shape, image_axis)
    text = lax.broadcasted_iota(jnp.int32, grad.shape, 1 - image_axis) - first
    return jnp.where((text == image) & (image < trows), grad - 1.0, grad)


def prepare(pictures_ref, partner_ref, images_ref):
    rows = pictures_ref.shape[0]
    images_ref[:rows, :] = normalized(pictures_ref[...])[0].astype(BF16)
    images_ref[rows:, :] = normalized(partner_ref[...])[0].astype(BF16)


def first_terms(device_ref, sharpness_ref, shift_ref, images_ref, near_ref, far_ref, near_part_ref, far_part_ref, *, trows):
    rows = near_ref.shape[0]
    texts = jnp.concatenate([near_ref[...], far_ref[...]], axis=0)
    grad = sigmoids(texts, images_ref[...], sharpness_ref[0], shift_ref[0])
    grad = less_pairs(grad, 1, trows * place_in_sheet(device_ref[0]), trows).astype(BF16)
    part = jnp.dot(grad, images_ref[...], preferred_element_type=F32)
    near_part_ref[...] = part[:rows]
    far_part_ref[...] = part[rows:].astype(BF16)


def far_terms(sharpness_ref, shift_ref, images_ref, *refs):
    n = len(refs) // 2
    rows = refs[0].shape[0]
    texts = jnp.concatenate([ref[...] for ref in refs[:n]], axis=0)
    grad = sigmoids(texts, images_ref[...], sharpness_ref[0], shift_ref[0]).astype(BF16)
    part = jnp.dot(grad, images_ref[...], preferred_element_type=F32)
    for k in range(n):
        refs[n + k][...] = part[k * rows : (k + 1) * rows].astype(BF16)


def near_sum(own_ref, far_ref, out_ref):
    out_ref[...] = own_ref[...] + far_ref[...].astype(F32)


def image_finish(device_ref, sharpness_ref, shift_ref, pictures_ref, *refs, trows):
    sharpness, shift = sharpness_ref[0], shift_ref[0]
    blocks = refs[: 2 * LINE]
    out_ref, raw, held, read_sem, sems = refs[2 * LINE :]
    read = pltpu.make_async_copy(pictures_ref, raw, read_sem)
    read.start()
    texts = jnp.concatenate([ref[...] for ref in blocks], axis=0)
    read.wait()
    tiles, tile = held.shape[:2]
    copies = []
    for k in range(tiles):
        rows = pl.ds(k * tile, tile)
        unit, scale = normalized(raw[rows, :])
        grad = sigmoids(unit.astype(BF16), texts, sharpness, shift)
        if k * tile < trows:
            grad = less_pairs(grad, 0, trows * place_in_sheet(device_ref[0]), trows)
        back = jnp.dot(grad.astype(BF16), texts, preferred_element_type=F32)
        held[k] = unit_backward(unit, scale, sharpness * back)
        copy = pltpu.make_async_copy(held.at[k], out_ref.at[rows, :], sems.at[k])
        copy.start()
        copies.append(copy)
    for copy in copies:
        copy.wait()


def line_sum(own_ref, *refs):
    out_ref = refs[-1]
    total = own_ref[...]
    for ref in refs[:-1]:
        total = total + ref[...].astype(F32)
    trows = out_ref.shape[1]
    for peer in range(out_ref.shape[0]):
        out_ref[peer] = total[peer * trows : (peer + 1) * trows].astype(BF16)


def text_finish(sharpness_ref, parts_ref, captions_ref, out_ref):
    total = parts_ref[0].astype(F32)
    for peer in range(1, parts_ref.shape[0]):
        total = total + parts_ref[peer].astype(F32)
    unit, scale = normalized(captions_ref[...])
    out_ref[...] = unit_backward(unit, scale, sharpness_ref[0] * total)


def routes():
    number = np.arange(256).reshape(2, 8, 2, 4, 2).transpose(4, 1, 2, 0, 3).reshape(2, 8, 4, 4)
    sheets = [number[0, :, :, x].reshape(-1) for x in range(4)] + [number[1, :, y, :].reshape(-1) for y in range(4)]
    lines = []
    for k in range(LINE):
        ahead = np.stack([np.roll(number[0], -k, axis=2), np.roll(number[1], -k, axis=1)])
        lines.append([(int(a), int(b)) for a, b in zip(number.reshape(-1), ahead.reshape(-1))])
    swap = [(int(i), int(i) ^ 1) for i in range(256)]
    return [[int(i) for i in sheet] for sheet in sheets], lines, swap


def on_device(pictures, captions, sharpness_factor, score_shift_constant):
    sheets, lines, swap = routes()
    trows, width = captions.shape
    rows = pictures.shape[0]
    n = len(sheets[0])
    block = n * trows
    shaped = jax.ShapeDtypeStruct

    def exchange(parts):
        return lax.all_to_all(parts, "d", 0, 0, axis_index_groups=sheets, tiled=True)

    with jax.named_scope("gather_texts"):
        partner = lax.ppermute(pictures, "d", swap)
        (sheet,) = call(text_units, [shaped((n, trows, width), BF16)], [VMEM], [captions])
        near = exchange(sheet).reshape(block, width)
        far = [lax.ppermute(near, "d", lines[k]) for k in (2, 1, 3)]
        far = far[1:] + far[:1]
        beside = [lax.ppermute(texts, "d", swap) for texts in (near, *far)]
    device = lax.axis_index("d").astype(jnp.int32).reshape(1)
    scalars = [sharpness_factor, score_shift_constant]
    low, part = shaped((2 * rows, width), BF16), shaped((block, width), BF16)
    work = dict(flops=8 * block * rows * width, transcendentals=2 * block * rows)
    with jax.named_scope("prepare"):
        (images,) = call(
            prepare,
            [low],
            [VMEM] * 2,
            [pictures, partner],
        )
    with jax.named_scope("far_terms"):
        near_part, p2 = call(
            functools.partial(first_terms, trows=trows),
            [shaped((block, width), F32), part],
            [SMEM] * 3 + [VMEM] * 3,
            [device, *scalars, images, near, far[2]],
            **work,
        )
        back = [lax.ppermute(p2, "d", lines[2])]
        p2, far[0] = lax.optimization_barrier((p2, far[0]))
        p1, p3 = call(far_terms, [part] * 2, [SMEM] * 2 + [VMEM] * 3, [*scalars, images, far[0], far[1]], **work)
        back += [lax.ppermute(p1, "d", lines[3]), lax.ppermute(p3, "d", lines[1])]
    with jax.named_scope("text_back"):
        (near_part,) = call(near_sum, [shaped((block, width), F32)], [VMEM] * 2, [near_part, back[0]])
        (total,) = call(line_sum, [shaped((n, trows, width), BF16)], [VMEM] * 3, [near_part, *back[1:]])
        sheet = exchange(total)
    with jax.named_scope("image_back"):
        tiles = 2
        (image_grad,) = call(
            functools.partial(image_finish, trows=trows),
            [shaped((rows, width), F32)],
            [SMEM] * 3 + [ANY] + [VMEM] * 8,
            [device, *scalars, pictures, near, *far, *beside],
            flops=16 * LINE * block * rows * width // 2,
            out_specs=[ANY],
            scratch_shapes=[
                pltpu.VMEM((rows, width), BF16),
                pltpu.VMEM((tiles, rows // tiles, width), F32),
                pltpu.SemaphoreType.DMA,
                pltpu.SemaphoreType.DMA((tiles,)),
            ],
        )
    with jax.named_scope("text_finish"):
        sheet, image_grad = lax.optimization_barrier((sheet, image_grad))
        (text_grad,) = call(
            text_finish,
            [shaped((trows, width), F32)],
            [SMEM, VMEM, VMEM],
            [sharpness_factor, sheet, captions],
        )
    return image_grad, text_grad


def solution(mesh):
    flat = Mesh(mesh.devices.reshape(-1), ("d",))
    whole = P("d", None)
    return jax.shard_map(
        on_device, mesh=flat, in_specs=(whole, whole, P(), P()), out_specs=(whole, whole), check_vma=False
    )
```

```python
import functools

import jax
import jax.numpy as jnp
import numpy as np
from jax import lax
from jax.experimental import pallas as pl
from jax.experimental.pallas import tpu as pltpu
from jax.sharding import Mesh, PartitionSpec as P

VMEM = pl.BlockSpec(memory_space=pltpu.VMEM)
ANY = pl.BlockSpec(memory_space=pl.ANY)
SMEM = pl.BlockSpec(memory_space=pltpu.SMEM)
CONTRACT_LAST = (((1,), (1,)), ((), ()))
BF16, F32 = jnp.bfloat16, jnp.float32
LINE = 4


def normalized(embeds):
    values = embeds.astype(F32)
    inverse_norm = lax.rsqrt(jnp.sum(values * values, axis=-1, keepdims=True) + 1e-06)
    return (values * inverse_norm, inverse_norm)


def unit_backward(normed, inverse_norm, upstream):
    along = jnp.sum(normed * upstream, axis=-1, keepdims=True)
    return inverse_norm * (upstream - normed * along)


def call(kernel, outs, in_specs, args, flops=0, transcendentals=0, vmem=16 << 20, **more):
    moved = sum(a.size * a.dtype.itemsize for a in args) + sum(o.size * o.dtype.itemsize for o in outs)
    more.setdefault("out_specs", [VMEM] * len(outs))
    return pl.pallas_call(
        kernel,
        out_shape=outs,
        in_specs=in_specs,
        compiler_params=pltpu.CompilerParams(vmem_limit_bytes=vmem),
        cost_estimate=pl.CostEstimate(flops=flops, bytes_accessed=moved, transcendentals=transcendentals),
        **more,
    )(*args)


def text_units(captions_ref, out_ref, unit_ref, scale_ref):
    unit, scale = normalized(captions_ref[...])
    unit_ref[...] = unit
    scale_ref[...] = jnp.broadcast_to(scale, scale_ref.shape)
    low = unit.astype(BF16)
    for peer in range(out_ref.shape[0]):
        out_ref[peer] = low


def place_in_sheet(device):
    y, z, x = 2 * (device // 8 % 2) + device // 128, device // 16 % 8, device // 2 % 4
    return 4 * z + jnp.where(device % 2 == 0, y, x)


def sigmoids(rows, columns, sharpness, shift):
    raw = lax.dot_general(rows, columns, CONTRACT_LAST, preferred_element_type=F32)
    return 1.0 / (1.0 + jnp.exp(-(sharpness * raw + shift)))


def less_pairs(grad, image_axis, first, trows):
    image = lax.broadcasted_iota(jnp.int32, grad.shape, image_axis)
    text = lax.broadcasted_iota(jnp.int32, grad.shape, 1 - image_axis) - first
    return jnp.where((text == image) & (image < trows), grad - 1.0, grad)


def prepare(pictures_ref, partner_ref, images_ref):
    rows = pictures_ref.shape[0]
    images_ref[:rows, :] = normalized(pictures_ref[...])[0].astype(BF16)
    images_ref[rows:, :] = normalized(partner_ref[...])[0].astype(BF16)


def first_terms(device_ref, sharpness_ref, shift_ref, images_ref, near_ref, far_ref, near_part_ref, far_part_ref, *, trows):
    rows = near_ref.shape[0]
    texts = jnp.concatenate([near_ref[...], far_ref[...]], axis=0)
    grad = sigmoids(texts, images_ref[...], sharpness_ref[0], shift_ref[0])
    grad = less_pairs(grad, 1, trows * place_in_sheet(device_ref[0]), trows).astype(BF16)
    part = jnp.dot(grad, images_ref[...], preferred_element_type=F32)
    near_part_ref[...] = part[:rows]
    far_part_ref[...] = part[rows:].astype(BF16)


def far_terms(sharpness_ref, shift_ref, images_ref, *refs):
    n = len(refs) // 2
    rows = refs[0].shape[0]
    texts = jnp.concatenate([ref[...] for ref in refs[:n]], axis=0)
    grad = sigmoids(texts, images_ref[...], sharpness_ref[0], shift_ref[0]).astype(BF16)
    part = jnp.dot(grad, images_ref[...], preferred_element_type=F32)
    for k in range(n):
        refs[n + k][...] = part[k * rows : (k + 1) * rows].astype(BF16)


def near_sum(own_ref, far_ref, out_ref):
    out_ref[...] = own_ref[...] + far_ref[...].astype(F32)


def image_finish(device_ref, sharpness_ref, shift_ref, pictures_ref, *refs, trows):
    sharpness, shift = sharpness_ref[0], shift_ref[0]
    blocks = refs[: 2 * LINE]
    out_ref, raw, held, read_sem, sems = refs[2 * LINE :]
    read = pltpu.make_async_copy(pictures_ref, raw, read_sem)
    read.start()
    texts = jnp.concatenate([ref[...] for ref in blocks], axis=0)
    read.wait()
    tiles, tile = held.shape[:2]
    copies = []
    for k in range(tiles):
        rows = pl.ds(k * tile, tile)
        unit, scale = normalized(raw[rows, :])
        grad = sigmoids(unit.astype(BF16), texts, sharpness, shift)
        if k * tile < trows:
            grad = less_pairs(grad, 0, trows * place_in_sheet(device_ref[0]), trows)
        back = jnp.dot(grad.astype(BF16), texts, preferred_element_type=F32)
        held[k] = unit_backward(unit, scale, sharpness * back)
        copy = pltpu.make_async_copy(held.at[k], out_ref.at[rows, :], sems.at[k])
        copy.start()
        copies.append(copy)
    for copy in copies:
        copy.wait()


def line_sum(own_ref, *refs):
    out_ref = refs[-1]
    total = own_ref[...]
    for ref in refs[:-1]:
        total = total + ref[...].astype(F32)
    trows = out_ref.shape[1]
    for peer in range(out_ref.shape[0]):
        out_ref[peer] = total[peer * trows : (peer + 1) * trows].astype(BF16)


def text_finish(sharpness_ref, parts_ref, unit_ref, scale_ref, out_ref):
    total = parts_ref[0].astype(F32)
    for peer in range(1, parts_ref.shape[0]):
        total = total + parts_ref[peer].astype(F32)
    out_ref[...] = unit_backward(unit_ref[...], scale_ref[:, :1], sharpness_ref[0] * total)


def routes():
    number = np.arange(256).reshape(2, 8, 2, 4, 2).transpose(4, 1, 2, 0, 3).reshape(2, 8, 4, 4)
    sheets = [number[0, :, :, x].reshape(-1) for x in range(4)] + [number[1, :, y, :].reshape(-1) for y in range(4)]
    lines = []
    for k in range(LINE):
        ahead = np.stack([np.roll(number[0], -k, axis=2), np.roll(number[1], -k, axis=1)])
        lines.append([(int(a), int(b)) for a, b in zip(number.reshape(-1), ahead.reshape(-1))])
    swap = [(int(i), int(i) ^ 1) for i in range(256)]
    return [[int(i) for i in sheet] for sheet in sheets], lines, swap


def on_device(pictures, captions, sharpness_factor, score_shift_constant):
    sheets, lines, swap = routes()
    trows, width = captions.shape
    rows = pictures.shape[0]
    n = len(sheets[0])
    block = n * trows
    shaped = jax.ShapeDtypeStruct

    def exchange(parts):
        return lax.all_to_all(parts, "d", 0, 0, axis_index_groups=sheets, tiled=True)

    with jax.named_scope("gather_texts"):
        partner = lax.ppermute(pictures, "d", swap)
        sheet, text_unit, text_scale = call(
            text_units,
            [shaped((n, trows, width), BF16), shaped((trows, width), F32), shaped((trows, 128), F32)],
            [VMEM],
            [captions],
        )
        near = exchange(sheet).reshape(block, width)
        far = [lax.ppermute(near, "d", lines[k]) for k in (2, 1, 3)]
        far = far[1:] + far[:1]
        beside = [lax.ppermute(texts, "d", swap) for texts in (near, *far)]
    device = lax.axis_index("d").astype(jnp.int32).reshape(1)
    scalars = [sharpness_factor, score_shift_constant]
    low, part = shaped((2 * rows, width), BF16), shaped((block, width), BF16)
    work = dict(flops=8 * block * rows * width, transcendentals=2 * block * rows)
    with jax.named_scope("prepare"):
        (images,) = call(
            prepare,
            [low],
            [VMEM] * 2,
            [pictures, partner],
        )
    with jax.named_scope("far_terms"):
        near_part, p2 = call(
            functools.partial(first_terms, trows=trows),
            [shaped((block, width), F32), part],
            [SMEM] * 3 + [VMEM] * 3,
            [device, *scalars, images, near, far[2]],
            **work,
        )
        back = [lax.ppermute(p2, "d", lines[2])]
        p2, far[0] = lax.optimization_barrier((p2, far[0]))
        p1, p3 = call(far_terms, [part] * 2, [SMEM] * 2 + [VMEM] * 3, [*scalars, images, far[0], far[1]], **work)
        back += [lax.ppermute(p1, "d", lines[3]), lax.ppermute(p3, "d", lines[1])]
    with jax.named_scope("text_back"):
        (near_part,) = call(near_sum, [shaped((block, width), F32)], [VMEM] * 2, [near_part, back[0]])
        (total,) = call(line_sum, [shaped((n, trows, width), BF16)], [VMEM] * 3, [near_part, *back[1:]])
        sheet = exchange(total)
    with jax.named_scope("image_back"):
        tiles = 2
        (image_grad,) = call(
            functools.partial(image_finish, trows=trows),
            [shaped((rows, width), F32)],
            [SMEM] * 3 + [ANY] + [VMEM] * 8,
            [device, *scalars, pictures, near, *far, *beside],
            flops=16 * LINE * block * rows * width // 2,
            out_specs=[ANY],
            scratch_shapes=[
                pltpu.VMEM((rows, width), BF16),
                pltpu.VMEM((tiles, rows // tiles, width), F32),
                pltpu.SemaphoreType.DMA,
                pltpu.SemaphoreType.DMA((tiles,)),
            ],
        )
    with jax.named_scope("text_finish"):
        sheet, image_grad = lax.optimization_barrier((sheet, image_grad))
        (text_grad,) = call(
            text_finish,
            [shaped((trows, width), F32)],
            [SMEM] + [VMEM] * 3,
            [sharpness_factor, sheet, text_unit, text_scale],
        )
    return image_grad, text_grad


def solution(mesh):
    flat = Mesh(mesh.devices.reshape(-1), ("d",))
    whole = P("d", None)
    return jax.shard_map(
        on_device, mesh=flat, in_specs=(whole, whole, P(), P()), out_specs=(whole, whole), check_vma=False
    )
```
